256 devices in a mesh: outer: 16 (over x_hi, z), inner: 16 (over x_lo, y, core).
Axes of the slice: x: 4 (x_hi: 2, x_lo: 2; x = x_hi * 2 + x_lo), y: 4, z: 8, core: 2. Of those that a mesh axis runs over, the one named last changes fastest.
Arguments:
- queries: bfloat16 [524288, 768], P(('outer', 'inner')), may hold values from -24 to 24
- keys: bfloat16 [524288, 768], P(('outer', 'inner')), may hold values from -24 to 24
- values: bfloat16 [524288, 768], P(('outer', 'inner')), may hold values from -6 to 6
- offset_mid: int32 [12], replicated, may hold values from 0 to 15
- offset_far: int32 [12], replicated, may hold values from 0 to 255
Outputs:
- attended: bfloat16 [524288, 768], P(('outer', 'inner'))
The draws below stay inside these ranges and needn't reach their ends.
All inputs are finite; a program needn't handle non-finite values.
Results may differ from the reference program's by a relative error of at most 0.0026.
Values may be sent and summed in bfloat16 or wider, within the bound.
No kernel may reach another device: no remote copies, remote signals or barrier semaphores. Data moves between devices by JAX's collectives and lax.ppermute only.
A program may use at most 128 MiB of HBM per device.

```python
import jax
import jax.numpy as jnp
from jax import lax

D = 768
HEADS = 12
HEAD_DIM = 64
TOK_DEV = 2048
TOKENS = 524288
R_MID = 16
R_FAR = 256
N_OUTER = 16


def draw_queries(key, part):
    key = jax.random.fold_in(key, 7)
    field = jnp.clip(2.0 * jax.random.normal(key, (TOKENS, HEADS * HEAD_DIM), jnp.float32), -12.0, 12.0)
    return field.astype(jnp.bfloat16)


def draw_keys(key, part):
    key = jax.random.fold_in(key, 9)
    field = jnp.clip(2.0 * jax.random.normal(key, (TOKENS, HEADS * HEAD_DIM), jnp.float32), -12.0, 12.0)
    return field.astype(jnp.bfloat16)


def place_ends(entries, key, least, largest):
    spot = [jax.random.randint(jax.random.fold_in(key, axis), (), 0, length) for axis, length in enumerate(entries.shape)]
    main_axis = entries.shape.index(max(entries.shape))
    beside = spot[:main_axis] + [(spot[main_axis] + 1) % entries.shape[main_axis]] + spot[main_axis + 1:]
    return entries.at[tuple(spot)].set(least).at[tuple(beside)].set(largest)


def steps_of(key, dims, split, least, top_value):
    loudness = 1.0
    for axis_at, parts in split:
        draws = jax.random.uniform(jax.random.fold_in(jax.random.fold_in(key, 6), axis_at), (parts,), jnp.float32, least / len(split), top_value / len(split))
        loudness = loudness * jnp.repeat(jnp.exp(draws), dims[axis_at] // parts).reshape((-1,) + (1,) * (len(dims) - 1 - axis_at))
    return loudness


def bell_draw(rng, dims, deviation, bound, shards=(), held_as=jnp.bfloat16):
    factor_of = steps_of(rng, dims, shards, -0.22, 0.18) if shards else 1.0
    drawn = jax.random.normal(rng, dims, jnp.float32) * deviation * factor_of
    return jnp.minimum(jnp.maximum(drawn, -bound), bound).astype(held_as)


def setup_inputs(seed: int = 0) -> dict:
    key_of = jax.random.split(jax.random.key(seed), 6)
    return {
        "queries": draw_queries(jax.random.fold_in(key_of[5], 71), 0),
        "keys": draw_keys(jax.random.fold_in(key_of[5], 71), 0),
        "values": bell_draw(key_of[2], (TOKENS, D), 1.0, 6.0, ((0, 256),)),
        "offset_mid": place_ends(jax.random.randint(key_of[3], (HEADS,), 0, R_MID), jax.random.fold_in(key_of[3], 1), 0, R_MID - 1).astype(jnp.int32),
        "offset_far": place_ends(jax.random.randint(key_of[4], (HEADS,), 0, R_FAR), jax.random.fold_in(key_of[4], 1), 0, R_FAR - 1).astype(jnp.int32),
    }


def attend(q3, k3, v3):
    scale = HEAD_DIM ** -0.5
    scores = jnp.einsum("qhd,khd->qhk", q3.astype(jnp.float32), k3.astype(jnp.float32)) * scale
    peak = jnp.max(scores, axis=-1)
    probs = jnp.exp(scores - peak[..., None])
    total = jnp.sum(probs, axis=-1)
    rounded = probs.astype(jnp.bfloat16).astype(jnp.float32)
    partial_sum = jnp.einsum("qhk,khd->qhd", rounded, v3.astype(jnp.float32))
    return peak, total, partial_sum


def pick_rows(field, stride, offsets):
    grid = field.reshape(-1, stride, HEADS, HEAD_DIM)
    return grid[:, offsets, jnp.arange(HEADS), :]


def spread(field, stride):
    count = field.shape[0]
    wide = jnp.broadcast_to(field[:, None], (count, stride) + field.shape[1:])
    return wide.reshape((count * stride,) + field.shape[1:])


def reference(queries, keys, values, offset_mid, offset_far):
    q_mid = pick_rows(queries, R_MID, offset_mid).reshape(N_OUTER, TOK_DEV, HEADS, HEAD_DIM)
    k_mid = pick_rows(keys, R_MID, offset_mid).reshape(N_OUTER, TOK_DEV, HEADS, HEAD_DIM)
    v_mid = pick_rows(values, R_MID, offset_mid).reshape(N_OUTER, TOK_DEV, HEADS, HEAD_DIM)
    peak_mid, total_mid, part_mid = lax.map(lambda trio: attend(trio[0], trio[1], trio[2]), (q_mid, k_mid, v_mid))
    blocks = TOKENS // TOK_DEV
    peak_mid = peak_mid.reshape(blocks, TOK_DEV // R_MID, HEADS)
    total_mid = total_mid.reshape(blocks, TOK_DEV // R_MID, HEADS)
    part_mid = part_mid.reshape(blocks, TOK_DEV // R_MID, HEADS, HEAD_DIM)
    peak_far, total_far, part_far = attend(pick_rows(queries, R_FAR, offset_far), pick_rows(keys, R_FAR, offset_far), pick_rows(values, R_FAR, offset_far))
    peak_far = peak_far.reshape(blocks, TOK_DEV // R_FAR, HEADS)
    total_far = total_far.reshape(blocks, TOK_DEV // R_FAR, HEADS)
    part_far = part_far.reshape(blocks, TOK_DEV // R_FAR, HEADS, HEAD_DIM)
    positions = jnp.arange(TOK_DEV)
    chosen_mid = (positions % R_MID)[:, None] == offset_mid[None, :]
    chosen_far = (positions % R_FAR)[:, None] == offset_far[None, :]

    def one_block(items):
        q_blk, k_blk, v_blk, pm, tm, am, pf, tf, af = items
        shape3 = (TOK_DEV, HEADS, HEAD_DIM)
        peak_loc, total_loc, part_loc = attend(q_blk.reshape(shape3), k_blk.reshape(shape3), v_blk.reshape(shape3))
        pm, tm, am = spread(pm, R_MID), spread(tm, R_MID), spread(am, R_MID)
        pf, tf, af = spread(pf, R_FAR), spread(tf, R_FAR), spread(af, R_FAR)
        top = jnp.maximum(peak_loc, jnp.where(chosen_mid, pm, peak_loc))
        top = jnp.maximum(top, jnp.where(chosen_far, pf, peak_loc))
        w_loc = jnp.exp(peak_loc - top)
        w_mid = jnp.where(chosen_mid, jnp.exp(pm - top), jnp.float32(0.0))
        w_far = jnp.where(chosen_far, jnp.exp(pf - top), jnp.float32(0.0))
        numer = w_loc[..., None] * part_loc + w_mid[..., None] * am + w_far[..., None] * af
        denom = w_loc * total_loc + w_mid * tm + w_far * tf
        return (numer / denom[..., None]).reshape(TOK_DEV, HEADS * HEAD_DIM).astype(jnp.bfloat16)

    width = HEADS * HEAD_DIM
    out = lax.map(one_block, (queries.reshape(blocks, TOK_DEV, width), keys.reshape(blocks, TOK_DEV, width), values.reshape(blocks, TOK_DEV, width), peak_mid, total_mid, part_mid, peak_far, total_far, part_far))
    return out.reshape(TOKENS, width)
```

```python
import functools

import jax
import jax.numpy as jnp
from jax import lax
from jax.experimental import pallas as pl
from jax.experimental.pallas import tpu as pltpu
from jax.sharding import PartitionSpec as P


NT = (((1,), (1,)), ((), ()))
LOG2E = 1.4426950408889634
SLOTS = 16
PAD = 256
PARTS = (2, 3, 1)
VMEM_LIMIT = 56 * 2**20


def scaled_queries(q):
    scaled = q.astype(jnp.float32) * (q.shape[1] ** -0.5 * LOG2E)
    high = scaled.astype(jnp.bfloat16)
    low = (scaled - high.astype(jnp.float32)).astype(jnp.bfloat16)
    return jnp.concatenate([high, low], 1)


def twice(x):
    return jnp.concatenate([x, x], 1)


def with_ones(v):
    return jnp.concatenate([v, jnp.ones_like(v)], 1)


def scores_of(q2, k2):
    return lax.dot_general(q2, k2, NT, preferred_element_type=jnp.float32)


def finish(acc, shift):
    half = acc.shape[1] // 2
    lane = lax.broadcasted_iota(jnp.int32, acc.shape, 1)
    return jnp.where(lane < half, acc / pltpu.roll(acc, half, 1), shift + jnp.log2(acc))


def attend_exact(q2, k2, v2):
    scores = scores_of(q2, k2)
    peak = jnp.max(scores, axis=1, keepdims=True)
    probs = jnp.exp2(scores - peak).astype(jnp.bfloat16)
    return finish(jnp.dot(probs, v2, preferred_element_type=jnp.float32), peak)


def attend_turned(q2, k2, vt, step):
    acc = None
    for j in range(k2.shape[0] // step):
        at = slice(j * step, (j + 1) * step)
        scores = scores_of(k2[at], q2)
        if j == 0:
            shift = jnp.max(scores, axis=0, keepdims=True)
        probs = jnp.exp2(scores - shift).astype(jnp.bfloat16)
        term = jnp.dot(vt[:, at], probs, preferred_element_type=jnp.float32)
        acc = term if acc is None else acc + term
    return acc, shift


def turned_values(v):
    return jnp.concatenate([v.T, jnp.ones((16, v.shape[0]), v.dtype)], 0)


def too_large(acc):
    return jnp.max(jnp.where(acc[64:72] < 2.0**100, 0.0, 1.0)) > 0.0


def parts_of(acc, shift):
    total = acc[64:65]
    return acc[:64] / total, jnp.broadcast_to(shift + jnp.log2(total), (64, acc.shape[1]))


def pick_kernel(om_ref, of_ref, q_ref, k_ref, v_ref, o_ref, scr):
    pair = pl.program_id(0)
    rows = q_ref.shape[0]
    half = q_ref.shape[1] // 2
    heads = om_ref.shape[0]
    got = []
    for n, ref in enumerate((q_ref, k_ref, v_ref)):
        scr[n, :rows] = ref[...].astype(jnp.float32)
    for h in range(2):
        head = jnp.minimum(2 * pair + h, heads - 1)
        om, of = om_ref[head], of_ref[head]
        for lo, n_rows, start, stride in ((0, 128, om, 16), (128, 8, of, 256)):
            q, k, v = [
                scr[n, pl.ds(start, n_rows, stride=stride), :][:, h * half : (h + 1) * half]
                for n in range(3)
            ]
            block = jnp.concatenate([q, k, v, jnp.zeros_like(v)], 1)
            if n_rows % 16:
                block = jnp.concatenate([block, jnp.zeros_like(block)], 0)
            o_ref[h, lo : lo + block.shape[0], :] = block.astype(jnp.bfloat16)


def pick(om, of, q, k, v):
    rows, width = q.shape
    last = width // 128 - 1
    spec = pl.BlockSpec((rows, 128), lambda i: (0, jnp.minimum(i, last)))
    smem = pl.BlockSpec(memory_space=pltpu.SMEM)
    return pl.pallas_call(
        pick_kernel,
        out_shape=jax.ShapeDtypeStruct((SLOTS, 144, 256), jnp.bfloat16),
        grid=(SLOTS // 2,),
        in_specs=[smem, smem, spec, spec, spec],
        out_specs=pl.BlockSpec((2, 144, 256), lambda i: (i, 0, 0)),
        scratch_shapes=[pltpu.VMEM((3, rows + PAD, 128), jnp.float32)],
        compiler_params=pltpu.CompilerParams(vmem_limit_bytes=VMEM_LIMIT),
        cost_estimate=pl.CostEstimate(flops=0, bytes_accessed=12 * 2**20, transcendentals=0),
    )(om, of, q, k, v)


def local_kernel(first, step, om_ref, of_ref, q_ref, k_ref, v_ref, *rest):
    o_ref, sel_ref, k2, vt, part, logs = rest[-6:]
    pair = pl.program_id(0) + first
    rows = q_ref.shape[0]
    turned = v_ref[...].T
    ones = jnp.ones((16, rows), turned.dtype)
    done = []
    for h in range(2):
        k2[h] = twice(k_ref[:, 64 * h : 64 * h + 64])
        vt[h] = jnp.concatenate([turned[64 * h : 64 * h + 64], ones], 0)
        q2 = scaled_queries(q_ref[:, 64 * h : 64 * h + 64])
        done.append(attend_turned(q2, k2.at[h], vt.at[h], step))
    below, above = zip(*[parts_of(*pair_of) for pair_of in done])
    part[:rows, :] = jnp.concatenate(below, 0).T
    logs[:rows, :] = jnp.concatenate(above, 0).T

    @pl.when(jnp.logical_or(too_large(done[0][0]), too_large(done[1][0])))
    def _():
        @pl.loop(0, rows // 128)
        def _(i):
            at = pl.ds(pl.multiple_of(i * 128, 128), 128)
            one, two = [
                attend_exact(
                    scaled_queries(q_ref[at, 64 * h : 64 * h + 64]),
                    k2[h],
                    with_ones(v_ref[:, 64 * h : 64 * h + 64]),
                )
                for h in range(2)
            ]
            lane = lax.broadcasted_iota(jnp.int32, one.shape, 1)
            part[at, :] = jnp.where(lane < 64, one, pltpu.roll(two, 64, 1))
            logs[at, :] = jnp.where(lane < 64, pltpu.roll(one, 64, 1), two)

    o_ref[...] = part[:rows, :].astype(jnp.bfloat16)
    for h in range(2):
        om, of = om_ref[2 * pair + h], of_ref[2 * pair + h]
        for lo, at in ((0, pl.ds(om, 128, stride=16)), (128, pl.ds(of, 8, stride=256))):
            low, up = part[at, :], logs[at, :]
            lane = lax.broadcasted_iota(jnp.int32, low.shape, 1)
            low, up = (pltpu.roll(low, 64, 1), up) if h else (low, pltpu.roll(up, 64, 1))
            chosen = jnp.where(lane < 64, low, up)
            if lo:
                chosen = twice_rows(chosen)
            sel_ref[h, lo : lo + chosen.shape[0], :] = chosen


def twice_rows(x):
    return jnp.concatenate([x, x], 0)


def local(first, count, om, of, q, k, v, out=None, sel=None):
    rows, width = q.shape
    spec = pl.BlockSpec((rows, 128), lambda i: (0, i + first))
    smem = pl.BlockSpec(memory_space=pltpu.SMEM)
    hbm = pl.BlockSpec(memory_space=pl.ANY)
    extra = () if out is None else (out, sel)
    return pl.pallas_call(
        functools.partial(local_kernel, first, 256),
        out_shape=[
            jax.ShapeDtypeStruct((rows, width), jnp.bfloat16),
            jax.ShapeDtypeStruct((width // 64, 144, 128), jnp.float32),
        ],
        grid=(count,),
        in_specs=[smem, smem, spec, spec, spec] + [hbm] * len(extra),
        out_specs=[spec, pl.BlockSpec((2, 144, 128), lambda i: (i + first, 0, 0))],
        scratch_shapes=[
            pltpu.VMEM((2, rows, 128), jnp.bfloat16),
            pltpu.VMEM((2, 80, rows), jnp.bfloat16),
            pltpu.VMEM((rows + PAD, 128), jnp.float32),
            pltpu.VMEM((rows + PAD, 128), jnp.float32),
        ],
        input_output_aliases={5: 0, 6: 1} if extra else {},
        compiler_params=pltpu.CompilerParams(vmem_limit_bytes=VMEM_LIMIT),
        cost_estimate=pl.CostEstimate(
            flops=count * 2 * 8 * 64 * rows * rows,
            bytes_accessed=count * 8 * rows * 128,
            transcendentals=count * 2 * rows * rows,
        ),
    )(om, of, q, k, v, *extra)


def cross_kernel(got_ref, far_ref, res_ref, k2, v2):
    groups = got_ref.shape[0]
    for j in range(groups):
        at = pl.ds(j * 128, 128)
        k2[at, :] = twice(got_ref[j, :128, 64:128])
        v2[at, :] = with_ones(got_ref[j, :128, 128:192])

    q2 = jnp.concatenate([scaled_queries(got_ref[j, :128, 0:64]) for j in range(groups)], 0)
    acc, shift = attend_turned(q2, k2, turned_values(v2[:, :64]), 256)
    below, above = parts_of(acc, shift)
    done = jnp.concatenate([below, above], 0).T
    for j in range(groups):
        res_ref[j, :128, :] = done[128 * j : 128 * (j + 1)]

    @pl.when(too_large(acc))
    def _():
        @pl.loop(0, groups)
        def _(i):
            res_ref[i, :128, :] = attend_exact(scaled_queries(got_ref[i, :128, 0:64]), k2[...], v2[...])

    for j in range(far_ref.shape[0]):
        at = pl.ds(j * 128, 128)
        k2[at, :] = twice(far_ref[j, :, 0:64])
        v2[at, :] = with_ones(far_ref[j, :, 64:128])
    n_far = far_ref.shape[0] * 128
    q2 = jnp.concatenate([scaled_queries(got_ref[j, 128:144, 0:64]) for j in range(groups)], 0)
    done = attend_exact(q2, k2[:n_far], v2[:n_far])
    for j in range(groups):
        res_ref[j, 128:144, :] = done[16 * j : 16 * (j + 1)]


def cross(got, far):
    groups = got.shape[0]
    return pl.pallas_call(
        cross_kernel,
        out_shape=jax.ShapeDtypeStruct((groups, 144, 128), jnp.float32),
        scratch_shapes=[
            pltpu.VMEM((groups * 128, 128), jnp.bfloat16),
            pltpu.VMEM((groups * 128, 128), jnp.bfloat16),
        ],
        compiler_params=pltpu.CompilerParams(vmem_limit_bytes=VMEM_LIMIT),
        cost_estimate=pl.CostEstimate(
            flops=8 * 64 * 2048 * 2304, bytes_accessed=4 * 2**20, transcendentals=2048 * 2304
        ),
    )(got, far)


def combine(a, b):
    half = a.shape[1] // 2
    lane = lax.broadcasted_iota(jnp.int32, a.shape, 1)
    top = jnp.maximum(a, b)
    wa, wb = jnp.exp2(a - top), jnp.exp2(b - top)
    total = wa + wb
    wa, wb = pltpu.roll(wa, half, 1), pltpu.roll(wb, half, 1)
    return jnp.where(lane < half, (wa * a + wb * b) / (wa + wb), top + jnp.log2(total))


def merge_kernel(om_ref, of_ref, back_ref, sel_ref, out_in_ref, out_ref, scr, mid):
    pair = pl.program_id(0)
    rows = out_in_ref.shape[0]
    scr[:rows, :] = out_in_ref[...].astype(jnp.float32)
    for h in range(2):
        om, of = om_ref[2 * pair + h], of_ref[2 * pair + h]
        mid[:128, :] = combine(sel_ref[h, :128, :], back_ref[h, :128, :])
        chosen = jnp.full((8, 128), of % 16 == om)
        base = jnp.where(chosen, mid[pl.ds(of // 16, 8, stride=16), :], sel_ref[h, 128:136, :])
        far = combine(base, back_ref[h, 128:136, :])
        for new, at in ((mid[:128, :], pl.ds(om, 128, stride=16)), (far, pl.ds(of, 8, stride=256))):
            lane = lax.broadcasted_iota(jnp.int32, new.shape, 1)
            if h:
                new = pltpu.roll(new, 64, 1)
            scr[at, :] = jnp.where((lane < 64) == (h == 0), new, scr[at, :])
    out_ref[...] = scr[:rows, :].astype(jnp.bfloat16)


def merge(om, of, back, sel, out):
    rows, width = out.shape
    spec = pl.BlockSpec((rows, 128), lambda i: (0, i))
    part = pl.BlockSpec((2, 144, 128), lambda i: (i, 0, 0))
    smem = pl.BlockSpec(memory_space=pltpu.SMEM)
    return pl.pallas_call(
        merge_kernel,
        out_shape=jax.ShapeDtypeStruct((rows, width), jnp.bfloat16),
        grid=(width // 128,),
        in_specs=[smem, smem, part, part, spec],
        out_specs=spec,
        scratch_shapes=[
            pltpu.VMEM((rows + PAD, 128), jnp.float32),
            pltpu.VMEM((128 + 16, 128), jnp.float32),
        ],
        input_output_aliases={4: 0},
        compiler_params=pltpu.CompilerParams(vmem_limit_bytes=VMEM_LIMIT),
        cost_estimate=pl.CostEstimate(flops=0, bytes_accessed=8 * 2**20, transcendentals=0),
    )(om, of, back, sel, out)


def per_device(queries, keys, values, offset_mid, offset_far):
    args = (offset_mid, offset_far, queries, keys, values)
    send = pick(*args)
    got = lax.all_to_all(send, "inner", 0, 0)
    out, sel = local(0, PARTS[0], *args)
    got, out, sel = lax.optimization_barrier((got, out, sel))
    outer = lax.axis_size("outer")
    far = got[:, 128:136, 64:192].reshape(128, 128)
    far = lax.all_to_all(jnp.broadcast_to(far, (outer, 128, 128)), "outer", 0, 0)
    out, sel = local(PARTS[0], PARTS[1], *args, out, sel)
    far, out, sel = lax.optimization_barrier((far, out, sel))
    back = lax.all_to_all(cross(got, far), "inner", 0, 0)
    out, sel = local(PARTS[0] + PARTS[1], PARTS[2], *args, out, sel)
    return merge(offset_mid, offset_far, back, sel, out)


def solution(mesh):
    split = P(("outer", "inner"), None)
    return jax.shard_map(
        per_device,
        mesh=mesh,
        in_specs=(split, split, split, P(), P()),
        out_specs=split,
        check_vma=False,
    )
```

```python
import functools

import jax
import jax.numpy as jnp
from jax import lax
from jax.experimental import pallas as pl
from jax.experimental.pallas import tpu as pltpu
from jax.sharding import PartitionSpec as P


NT = (((1,), (1,)), ((), ()))
LOG2E = 1.4426950408889634
SLOTS = 16
PAD = 256
PARTS = (2, 2, 2)
VMEM_LIMIT = 56 * 2**20


def scaled_queries(q):
    scaled = q.astype(jnp.float32) * (q.shape[1] ** -0.5 * LOG2E)
    high = scaled.astype(jnp.bfloat16)
    low = (scaled - high.astype(jnp.float32)).astype(jnp.bfloat16)
    return jnp.concatenate([high, low], 1)


def twice(x):
    return jnp.concatenate([x, x], 1)


def with_ones(v):
    return jnp.concatenate([v, jnp.ones_like(v)], 1)


def scores_of(q2, k2):
    return lax.dot_general(q2, k2, NT, preferred_element_type=jnp.float32)


def finish(acc, shift):
    half = acc.shape[1] // 2
    lane = lax.broadcasted_iota(jnp.int32, acc.shape, 1)
    return jnp.where(lane < half, acc / pltpu.roll(acc, half, 1), shift + jnp.log2(acc))


def attend_exact(q2, k2, v2):
    scores = scores_of(q2, k2)
    peak = jnp.max(scores, axis=1, keepdims=True)
    probs = jnp.exp2(scores - peak).astype(jnp.bfloat16)
    return finish(jnp.dot(probs, v2, preferred_element_type=jnp.float32), peak)


def attend_turned(q2, k2, vt, step):
    acc = None
    for j in range(k2.shape[0] // step):
        at = slice(j * step, (j + 1) * step)
        scores = scores_of(k2[at], q2)
        if j == 0:
            shift = jnp.max(scores, axis=0, keepdims=True)
        probs = jnp.exp2(scores - shift).astype(jnp.bfloat16)
        term = jnp.dot(vt[:, at], probs, preferred_element_type=jnp.float32)
        acc = term if acc is None else acc + term
    return acc, shift


def turned_values(v):
    return jnp.concatenate([v.T, jnp.ones((16, v.shape[0]), v.dtype)], 0)


def too_large(acc):
    return jnp.max(jnp.where(acc[64:72] < 2.0**100, 0.0, 1.0)) > 0.0


def parts_of(acc, shift):
    total = acc[64:65]
    return acc[:64] / total, jnp.broadcast_to(shift + jnp.log2(total), (64, acc.shape[1]))


def pick_kernel(om_ref, of_ref, q_ref, k_ref, v_ref, o_ref, scr):
    pair = pl.program_id(0)
    rows = q_ref.shape[0]
    half = q_ref.shape[1] // 2
    for n, ref in enumerate((q_ref, k_ref, v_ref)):
        scr[n, :rows] = ref[...].astype(jnp.float32)
    for h in range(2):
        om, of = om_ref[2 * pair + h], of_ref[2 * pair + h]
        for lo, n_rows, start, stride in ((0, 128, om, 16), (128, 8, of, 256)):
            q, k, v = [
                scr[n, pl.ds(start, n_rows, stride=stride), :][:, h * half : (h + 1) * half]
                for n in range(3)
            ]
            block = jnp.concatenate([q, k, v, jnp.zeros_like(v)], 1)
            if n_rows % 16:
                block = jnp.concatenate([block, jnp.zeros_like(block)], 0)
            o_ref[h, lo : lo + block.shape[0], :] = block.astype(jnp.bfloat16)


def pick(om, of, q, k, v):
    rows, width = q.shape
    spec = pl.BlockSpec((rows, 128), lambda i: (0, i))
    smem = pl.BlockSpec(memory_space=pltpu.SMEM)
    return pl.pallas_call(
        pick_kernel,
        out_shape=jax.ShapeDtypeStruct((SLOTS, 144, 256), jnp.bfloat16),
        grid=(width // 128,),
        in_specs=[smem, smem, spec, spec, spec],
        out_specs=pl.BlockSpec((2, 144, 256), lambda i: (i, 0, 0)),
        scratch_shapes=[pltpu.VMEM((3, rows + PAD, 128), jnp.float32)],
        compiler_params=pltpu.CompilerParams(vmem_limit_bytes=VMEM_LIMIT),
        cost_estimate=pl.CostEstimate(flops=0, bytes_accessed=12 * 2**20, transcendentals=0),
    )(om, of, q, k, v)


def local_kernel(first, step, om_ref, of_ref, q_ref, k_ref, v_ref, *rest):
    o_ref, sel_ref, k2, vt, part, logs = rest[-6:]
    pair = pl.program_id(0) + first
    rows = q_ref.shape[0]
    turned = v_ref[...].T
    ones = jnp.ones((16, rows), turned.dtype)
    done = []
    for h in range(2):
        k2[h] = twice(k_ref[:, 64 * h : 64 * h + 64])
        vt[h] = jnp.concatenate([turned[64 * h : 64 * h + 64], ones], 0)
        q2 = scaled_queries(q_ref[:, 64 * h : 64 * h + 64])
        done.append(attend_turned(q2, k2.at[h], vt.at[h], step))
    below, above = zip(*[parts_of(*pair_of) for pair_of in done])
    result = jnp.concatenate(below, 0).T
    part[:rows, :] = result
    o_ref[...] = result.astype(jnp.bfloat16)
    logs[:rows, :] = jnp.concatenate(above, 0).T

    @pl.when(jnp.logical_or(too_large(done[0][0]), too_large(done[1][0])))
    def _():
        @pl.loop(0, rows // 128)
        def _(i):
            at = pl.ds(pl.multiple_of(i * 128, 128), 128)
            one, two = [
                attend_exact(
                    scaled_queries(q_ref[at, 64 * h : 64 * h + 64]),
                    k2[h],
                    with_ones(v_ref[:, 64 * h : 64 * h + 64]),
                )
                for h in range(2)
            ]
            lane = lax.broadcasted_iota(jnp.int32, one.shape, 1)
            again = jnp.where(lane < 64, one, pltpu.roll(two, 64, 1))
            part[at, :] = again
            o_ref[at, :] = again.astype(jnp.bfloat16)
            logs[at, :] = jnp.where(lane < 64, pltpu.roll(one, 64, 1), two)

    for h in range(2):
        om, of = om_ref[2 * pair + h], of_ref[2 * pair + h]
        for lo, at in ((0, pl.ds(om, 128, stride=16)), (128, pl.ds(of, 8, stride=256))):
            low, up = part[at, :], logs[at, :]
            lane = lax.broadcasted_iota(jnp.int32, low.shape, 1)
            low, up = (pltpu.roll(low, 64, 1), up) if h else (low, pltpu.roll(up, 64, 1))
            chosen = jnp.where(lane < 64, low, up)
            if lo:
                chosen = twice_rows(chosen)
            sel_ref[h, lo : lo + chosen.shape[0], :] = chosen


def twice_rows(x):
    return jnp.concatenate([x, x], 0)


def local(first, count, om, of, q, k, v, out=None, sel=None):
    rows, width = q.shape
    spec = pl.BlockSpec((rows, 128), lambda i: (0, i + first))
    smem = pl.BlockSpec(memory_space=pltpu.SMEM)
    hbm = pl.BlockSpec(memory_space=pl.ANY)
    extra = () if out is None else (out, sel)
    return pl.pallas_call(
        functools.partial(local_kernel, first, 256),
        out_shape=[
            jax.ShapeDtypeStruct((rows, width), jnp.bfloat16),
            jax.ShapeDtypeStruct((width // 64, 144, 128), jnp.float32),
        ],
        grid=(count,),
        in_specs=[smem, smem, spec, spec, spec] + [hbm] * len(extra),
        out_specs=[spec, pl.BlockSpec((2, 144, 128), lambda i: (i + first, 0, 0))],
        scratch_shapes=[
            pltpu.VMEM((2, rows, 128), jnp.bfloat16),
            pltpu.VMEM((2, 80, rows), jnp.bfloat16),
            pltpu.VMEM((rows + PAD, 128), jnp.float32),
            pltpu.VMEM((rows + PAD, 128), jnp.float32),
        ],
        input_output_aliases={5: 0, 6: 1} if extra else {},
        compiler_params=pltpu.CompilerParams(vmem_limit_bytes=VMEM_LIMIT),
        cost_estimate=pl.CostEstimate(
            flops=count * 2 * 8 * 64 * rows * rows,
            bytes_accessed=count * 8 * rows * 128,
            transcendentals=count * 2 * rows * rows,
        ),
    )(om, of, q, k, v, *extra)


def cross_kernel(heads, slot_ref, got_ref, far_ref, res_ref, k2, v2):
    @pl.when(slot_ref[0] < heads)
    def _():
        cross_body(got_ref, far_ref, res_ref, k2, v2)


def cross_body(got_ref, far_ref, res_ref, k2, v2):
    groups = got_ref.shape[0]
    for j in range(groups):
        at = pl.ds(j * 128, 128)
        k2[at, :] = twice(got_ref[j, :128, 64:128])
        v2[at, :] = with_ones(got_ref[j, :128, 128:192])

    q2 = jnp.concatenate([scaled_queries(got_ref[j, :128, 0:64]) for j in range(groups)], 0)
    acc, shift = attend_turned(q2, k2, turned_values(v2[:, :64]), 256)
    below, above = parts_of(acc, shift)
    done = jnp.concatenate([below, above], 0).T
    for j in range(groups):
        res_ref[j, :128, :] = done[128 * j : 128 * (j + 1)]

    @pl.when(too_large(acc))
    def _():
        @pl.loop(0, groups)
        def _(i):
            res_ref[i, :128, :] = attend_exact(scaled_queries(got_ref[i, :128, 0:64]), k2[...], v2[...])

    for j in range(far_ref.shape[0]):
        at = pl.ds(j * 128, 128)
        k2[at, :] = twice(far_ref[j, :, 0:64])
        v2[at, :] = with_ones(far_ref[j, :, 64:128])
    n_far = far_ref.shape[0] * 128
    q2 = jnp.concatenate([scaled_queries(got_ref[j, 128:144, 0:64]) for j in range(groups)], 0)
    done = attend_exact(q2, k2[:n_far], v2[:n_far])
    for j in range(groups):
        res_ref[j, 128:144, :] = done[16 * j : 16 * (j + 1)]


def cross(heads, slot, got, far):
    groups = got.shape[0]
    vmem = pl.BlockSpec(memory_space=pltpu.VMEM)
    return pl.pallas_call(
        functools.partial(cross_kernel, heads),
        in_specs=[pl.BlockSpec(memory_space=pltpu.SMEM), vmem, vmem],
        out_specs=vmem,
        out_shape=jax.ShapeDtypeStruct((groups, 144, 128), jnp.float32),
        scratch_shapes=[
            pltpu.VMEM((groups * 128, 128), jnp.bfloat16),
            pltpu.VMEM((groups * 128, 128), jnp.bfloat16),
        ],
        compiler_params=pltpu.CompilerParams(vmem_limit_bytes=VMEM_LIMIT),
        cost_estimate=pl.CostEstimate(
            flops=8 * 64 * 2048 * 2304, bytes_accessed=4 * 2**20, transcendentals=2048 * 2304
        ),
    )(slot, got, far)


def combine(a, b):
    half = a.shape[1] // 2
    lane = lax.broadcasted_iota(jnp.int32, a.shape, 1)
    top = jnp.maximum(a, b)
    wa, wb = jnp.exp2(a - top), jnp.exp2(b - top)
    total = wa + wb
    wa, wb = pltpu.roll(wa, half, 1), pltpu.roll(wb, half, 1)
    return jnp.where(lane < half, (wa * a + wb * b) / (wa + wb), top + jnp.log2(total))


def merge_kernel(om_ref, of_ref, back_ref, sel_ref, out_in_ref, out_ref, scr, mid):
    pair = pl.program_id(0)
    rows = out_in_ref.shape[0]
    scr[:rows, :] = out_in_ref[...].astype(jnp.float32)
    for h in range(2):
        om, of = om_ref[2 * pair + h], of_ref[2 * pair + h]
        mid[:128, :] = combine(sel_ref[h, :128, :], back_ref[h, :128, :])
        chosen = jnp.full((8, 128), of % 16 == om)
        base = jnp.where(chosen, mid[pl.ds(of // 16, 8, stride=16), :], sel_ref[h, 128:136, :])
        far = combine(base, back_ref[h, 128:136, :])
        for new, at in ((mid[:128, :], pl.ds(om, 128, stride=16)), (far, pl.ds(of, 8, stride=256))):
            lane = lax.broadcasted_iota(jnp.int32, new.shape, 1)
            if h:
                new = pltpu.roll(new, 64, 1)
            scr[at, :] = jnp.where((lane < 64) == (h == 0), new, scr[at, :])
    out_ref[...] = scr[:rows, :].astype(jnp.bfloat16)


def merge(om, of, back, sel, out):
    rows, width = out.shape
    spec = pl.BlockSpec((rows, 128), lambda i: (0, i))
    part = pl.BlockSpec((2, 144, 128), lambda i: (i, 0, 0))
    smem = pl.BlockSpec(memory_space=pltpu.SMEM)
    return pl.pallas_call(
        merge_kernel,
        out_shape=jax.ShapeDtypeStruct((rows, width), jnp.bfloat16),
        grid=(width // 128,),
        in_specs=[smem, smem, part, part, spec],
        out_specs=spec,
        scratch_shapes=[
            pltpu.VMEM((rows + PAD, 128), jnp.float32),
            pltpu.VMEM((128 + 16, 128), jnp.float32),
        ],
        input_output_aliases={4: 0},
        compiler_params=pltpu.CompilerParams(vmem_limit_bytes=VMEM_LIMIT),
        cost_estimate=pl.CostEstimate(flops=0, bytes_accessed=8 * 2**20, transcendentals=0),
    )(om, of, back, sel, out)


def per_device(queries, keys, values, offset_mid, offset_far):
    args = (offset_mid, offset_far, queries, keys, values)
    send = pick(*args)
    got = lax.all_to_all(send, "inner", 0, 0)
    out, sel = local(0, PARTS[0], *args)
    got, out, sel = lax.optimization_barrier((got, out, sel))
    outer = lax.axis_size("outer")
    far = got[:, 128:136, 64:192].reshape(128, 128)
    far = lax.all_to_all(jnp.broadcast_to(far, (outer, 128, 128)), "outer", 0, 0)
    out, sel = local(PARTS[0], PARTS[1], *args, out, sel)
    far, out, sel = lax.optimization_barrier((far, out, sel))
    slot = lax.axis_index("inner").reshape(1)
    back = lax.all_to_all(cross(offset_mid.shape[0], slot, got, far), "inner", 0, 0)
    out, sel = local(PARTS[0] + PARTS[1], PARTS[2], *args, out, sel)
    return merge(offset_mid, offset_far, back, sel, out)


def solution(mesh):
    split = P(("outer", "inner"), None)
    return jax.shard_map(
        per_device,
        mesh=mesh,
        in_specs=(split, split, split, P(), P()),
        out_specs=split,
        check_vma=False,
    )
```

```python
import functools

import jax
import jax.numpy as jnp
from jax import lax
from jax.experimental import pallas as pl
from jax.experimental.pallas import tpu as pltpu
from jax.sharding import PartitionSpec as P


NT = (((1,), (1,)), ((), ()))
LOG2E = 1.4426950408889634
SLOTS = 16
PAD = 256
PARTS = (2, 2, 2)
VMEM_LIMIT = 56 * 2**20


def scaled_queries(q):
    scaled = q.astype(jnp.float32) * (q.shape[1] ** -0.5 * LOG2E)
    high = scaled.astype(jnp.bfloat16)
    low = (scaled - high.astype(jnp.float32)).astype(jnp.bfloat16)
    return jnp.concatenate([high, low], 1)


def twice(x):
    return jnp.concatenate([x, x], 1)


def with_ones(v):
    return jnp.concatenate([v, jnp.ones_like(v)], 1)


def scores_of(q2, k2):
    return lax.dot_general(q2, k2, NT, preferred_element_type=jnp.float32)


def finish(acc, shift):
    half = acc.shape[1] // 2
    lane = lax.broadcasted_iota(jnp.int32, acc.shape, 1)
    return jnp.where(lane < half, acc / pltpu.roll(acc, half, 1), shift + jnp.log2(acc))


def attend_exact(q2, k2, v2):
    scores = scores_of(q2, k2)
    peak = jnp.max(scores, axis=1, keepdims=True)
    probs = jnp.exp2(scores - peak).astype(jnp.bfloat16)
    return finish(jnp.dot(probs, v2, preferred_element_type=jnp.float32), peak)


def attend_turned(q2, k2, vt, step):
    acc = None
    for j in range(k2.shape[0] // step):
        at = slice(j * step, (j + 1) * step)
        scores = scores_of(k2[at], q2)
        if j == 0:
            shift = jnp.max(scores, axis=0, keepdims=True)
        probs = jnp.exp2(scores - shift).astype(jnp.bfloat16)
        term = jnp.dot(vt[:, at], probs, preferred_element_type=jnp.float32)
        acc = term if acc is None else acc + term
    return acc, shift


def turned_values(v):
    return jnp.concatenate([v.T, jnp.ones((16, v.shape[0]), v.dtype)], 0)


def too_large(*accs):
    flags = [jnp.where(acc[64:72] < 2.0**100, 0.0, 1.0) for acc in accs]
    return jnp.max(functools.reduce(jnp.maximum, flags)) > 0.0


def parts_of(acc, shift):
    total = acc[64:65]
    return acc[:64] * (1.0 / total), jnp.broadcast_to(shift + jnp.log2(total), (64, acc.shape[1]))


def pick_kernel(om_ref, of_ref, q_ref, k_ref, v_ref, o_ref, scr, far):
    step = pl.program_id(0)
    rows = q_ref.shape[0]
    n_mid, n_far = rows // 16, rows // 256
    for n, ref in enumerate((q_ref, k_ref, v_ref)):
        for p in range(ref.shape[1] // 128):
            scr[n, p, :rows] = ref[:, 128 * p : 128 * p + 128].astype(jnp.float32)

    def chosen(h, start, count, stride):
        q, k, v = [scr[n, h // 2, pl.ds(start, count, stride=stride), :] for n in range(3)]
        lane = lax.broadcasted_iota(jnp.int32, q.shape, 1)
        if h % 2:
            q, v = pltpu.roll(q, 64, 1), pltpu.roll(v, 64, 1)
        else:
            k = pltpu.roll(k, 64, 1)
        return jnp.concatenate([jnp.where(lane < 64, q, k), jnp.where(lane < 64, v, 0.0)], 1)

    for h in range(om_ref.shape[0]):
        at = pl.ds(pl.multiple_of(step * n_mid, n_mid), n_mid)
        o_ref[h, at, :] = chosen(h, om_ref[h], n_mid, 16).astype(jnp.bfloat16)
        far[step, h, :n_far, :] = chosen(h, of_ref[h], n_far, 256)

    @pl.when(step == pl.num_programs(0) - 1)
    def _():
        for h in range(om_ref.shape[0]):
            rows_of_head = jnp.concatenate([far[i, h, :n_far, :] for i in range(far.shape[0])], 0)
            o_ref[h, 128:, :] = twice_rows(rows_of_head).astype(jnp.bfloat16)


def pick(om, of, q, k, v):
    rows, width = q.shape
    block = 512
    spec = pl.BlockSpec((block, width), lambda i: (i, 0))
    smem = pl.BlockSpec(memory_space=pltpu.SMEM)
    return pl.pallas_call(
        pick_kernel,
        out_shape=jax.ShapeDtypeStruct((SLOTS, 144, 256), jnp.bfloat16),
        grid=(rows // block,),
        in_specs=[smem, smem, spec, spec, spec],
        out_specs=pl.BlockSpec((SLOTS, 144, 256), lambda i: (0, 0, 0)),
        scratch_shapes=[
            pltpu.VMEM((3, width // 128, block + PAD, 128), jnp.float32),
            pltpu.VMEM((rows // block, width // 64, 8, 256), jnp.float32),
        ],
        compiler_params=pltpu.CompilerParams(vmem_limit_bytes=VMEM_LIMIT),
        cost_estimate=pl.CostEstimate(flops=0, bytes_accessed=12 * 2**20, transcendentals=0),
    )(om, of, q, k, v)


def local_kernel(first, step, om_ref, of_ref, q_ref, k_ref, v_ref, *rest):
    o_ref, sel_ref, k2, vt, part, logs = rest[-6:]
    pair = pl.program_id(0) + first
    rows = q_ref.shape[0]
    turned = v_ref[...].T
    ones = jnp.ones((16, rows), turned.dtype)
    done = []
    for h in range(2):
        k2[h] = twice(k_ref[:, 64 * h : 64 * h + 64])
        vt[h] = jnp.concatenate([turned[64 * h : 64 * h + 64], ones], 0)
        q2 = scaled_queries(q_ref[:, 64 * h : 64 * h + 64])
        done.append(attend_turned(q2, k2.at[h], vt.at[h], step))
    below, above = zip(*[parts_of(*pair_of) for pair_of in done])
    result = jnp.concatenate(below, 0).T
    part[:rows, :] = result
    o_ref[...] = result.astype(jnp.bfloat16)
    logs[:rows, :] = jnp.concatenate(above, 0).T

    @pl.when(too_large(done[0][0], done[1][0]))
    def _():
        @pl.loop(0, rows // 128)
        def _(i):
            at = pl.ds(pl.multiple_of(i * 128, 128), 128)
            one, two = [
                attend_exact(
                    scaled_queries(q_ref[at, 64 * h : 64 * h + 64]),
                    k2[h],
                    with_ones(v_ref[:, 64 * h : 64 * h + 64]),
                )
                for h in range(2)
            ]
            lane = lax.broadcasted_iota(jnp.int32, one.shape, 1)
            again = jnp.where(lane < 64, one, pltpu.roll(two, 64, 1))
            part[at, :] = again
            o_ref[at, :] = again.astype(jnp.bfloat16)
            logs[at, :] = jnp.where(lane < 64, pltpu.roll(one, 64, 1), two)

    for h in range(2):
        om, of = om_ref[2 * pair + h], of_ref[2 * pair + h]
        for lo, at in ((0, pl.ds(om, 128, stride=16)), (128, pl.ds(of, 8, stride=256))):
            low, up = part[at, :], logs[at, :]
            lane = lax.broadcasted_iota(jnp.int32, low.shape, 1)
            low, up = (pltpu.roll(low, 64, 1), up) if h else (low, pltpu.roll(up, 64, 1))
            chosen = jnp.where(lane < 64, low, up)
            if lo:
                chosen = twice_rows(chosen)
            sel_ref[h, lo : lo + chosen.shape[0], :] = chosen


def twice_rows(x):
    return jnp.concatenate([x, x], 0)


def local(first, count, om, of, q, k, v, out=None, sel=None):
    rows, width = q.shape
    spec = pl.BlockSpec((rows, 128), lambda i: (0, i + first))
    smem = pl.BlockSpec(memory_space=pltpu.SMEM)
    hbm = pl.BlockSpec(memory_space=pl.ANY)
    extra = () if out is None else (out, sel)
    return pl.pallas_call(
        functools.partial(local_kernel, first, 256),
        out_shape=[
            jax.ShapeDtypeStruct((rows, width), jnp.bfloat16),
            jax.ShapeDtypeStruct((width // 64, 144, 128), jnp.float32),
        ],
        grid=(count,),
        in_specs=[smem, smem, spec, spec, spec] + [hbm] * len(extra),
        out_specs=[spec, pl.BlockSpec((2, 144, 128), lambda i: (i + first, 0, 0))],
        scratch_shapes=[
            pltpu.VMEM((2, rows, 128), jnp.bfloat16),
            pltpu.VMEM((2, 80, rows), jnp.bfloat16),
            pltpu.VMEM((rows + PAD, 128), jnp.float32),
            pltpu.VMEM((rows + PAD, 128), jnp.float32),
        ],
        input_output_aliases={5: 0, 6: 1} if extra else {},
        compiler_params=pltpu.CompilerParams(vmem_limit_bytes=VMEM_LIMIT),
        cost_estimate=pl.CostEstimate(
            flops=count * 2 * 8 * 64 * rows * rows,
            bytes_accessed=count * 8 * rows * 128,
            transcendentals=count * 2 * rows * rows,
        ),
    )(om, of, q, k, v, *extra)


def cross_kernel(heads, slot_ref, got_ref, far_ref, res_ref, k2, v2):
    @pl.when(slot_ref[0] < heads)
    def _():
        cross_body(got_ref, far_ref, res_ref, k2, v2)


def cross_body(got_ref, far_ref, res_ref, k2, v2):
    groups = got_ref.shape[0]
    for j in range(groups):
        at = pl.ds(j * 128, 128)
        k2[at, :] = twice(got_ref[j, :128, 64:128])
        v2[at, :] = with_ones(got_ref[j, :128, 128:192])

    q2 = jnp.concatenate([scaled_queries(got_ref[j, :128, 0:64]) for j in range(groups)], 0)
    acc, shift = attend_turned(q2, k2, turned_values(v2[:, :64]), 256)
    below, above = parts_of(acc, shift)
    done = jnp.concatenate([below, above], 0).T
    for j in range(groups):
        res_ref[j, :128, :] = done[128 * j : 128 * (j + 1)]

    @pl.when(too_large(acc))
    def _():
        @pl.loop(0, groups)
        def _(i):
            res_ref[i, :128, :] = attend_exact(scaled_queries(got_ref[i, :128, 0:64]), k2[...], v2[...])

    for j in range(far_ref.shape[0]):
        at = pl.ds(j * 128, 128)
        k2[at, :] = twice(far_ref[j, :, 0:64])
        v2[at, :] = with_ones(far_ref[j, :, 64:128])
    n_far = far_ref.shape[0] * 128
    rows = [got_ref[j, 128:144, 0:64].astype(jnp.float32)[:8] for j in range(groups)]
    q2 = scaled_queries(jnp.concatenate(rows, 0))
    done = attend_exact(q2, k2[:n_far], v2[:n_far])
    for j in range(groups):
        res_ref[j, 128:136, :] = done[8 * j : 8 * (j + 1)]
        res_ref[j, 136:144, :] = jnp.zeros((8, 128), jnp.float32)


def cross(heads, slot, got, far):
    groups = got.shape[0]
    vmem = pl.BlockSpec(memory_space=pltpu.VMEM)
    return pl.pallas_call(
        functools.partial(cross_kernel, heads),
        in_specs=[pl.BlockSpec(memory_space=pltpu.SMEM), vmem, vmem],
        out_specs=vmem,
        out_shape=jax.ShapeDtypeStruct((groups, 144, 128), jnp.float32),
        scratch_shapes=[
            pltpu.VMEM((groups * 128, 128), jnp.bfloat16),
            pltpu.VMEM((groups * 128, 128), jnp.bfloat16),
        ],
        compiler_params=pltpu.CompilerParams(vmem_limit_bytes=VMEM_LIMIT),
        cost_estimate=pl.CostEstimate(
            flops=8 * 64 * 2048 * 2304, bytes_accessed=4 * 2**20, transcendentals=2048 * 2304
        ),
    )(slot, got, far)


def combine(a, b):
    half = a.shape[1] // 2
    lane = lax.broadcasted_iota(jnp.int32, a.shape, 1)
    top = jnp.maximum(a, b)
    wa, wb = jnp.exp2(a - top), jnp.exp2(b - top)
    total = wa + wb
    wa, wb = pltpu.roll(wa, half, 1), pltpu.roll(wb, half, 1)
    return jnp.where(lane < half, (wa * a + wb * b) / (wa + wb), top + jnp.log2(total))


def merge_kernel(om_ref, of_ref, back_ref, sel_ref, out_in_ref, out_ref, scr, mid):
    rows = out_in_ref.shape[0]
    for p in range(2):
        scr[p, :rows, :] = out_in_ref[:, 128 * p : 128 * p + 128].astype(jnp.float32)
    for h in range(4):
        head = 4 * pl.program_id(0) + h
        om, of = om_ref[head], of_ref[head]
        merged = combine(sel_ref[h, :128, :], back_ref[h, :128, :])
        mid[h, :128, :] = merged
        chosen = jnp.full((8, 128), of % 16 == om)
        base = jnp.where(chosen, mid[h, pl.ds(of // 16, 8, stride=16), :], sel_ref[h, 128:136, :])
        far = combine(base, back_ref[h, 128:136, :])
        for new, at in ((merged, pl.ds(om, 128, stride=16)), (far, pl.ds(of, 8, stride=256))):
            lane = lax.broadcasted_iota(jnp.int32, new.shape, 1)
            if h % 2:
                new = pltpu.roll(new, 64, 1)
            scr[h // 2, at, :] = jnp.where((lane < 64) == (h % 2 == 0), new, scr[h // 2, at, :])
    for p in range(2):
        out_ref[:, 128 * p : 128 * p + 128] = scr[p, :rows, :].astype(jnp.bfloat16)


def merge(om, of, back, sel, out):
    rows, width = out.shape
    spec = pl.BlockSpec((rows, 256), lambda i: (0, i))
    part = pl.BlockSpec((4, 144, 128), lambda i: (i, 0, 0))
    smem = pl.BlockSpec(memory_space=pltpu.SMEM)
    return pl.pallas_call(
        merge_kernel,
        out_shape=jax.ShapeDtypeStruct((rows, width), jnp.bfloat16),
        grid=(width // 256,),
        in_specs=[smem, smem, part, part, spec],
        out_specs=spec,
        scratch_shapes=[
            pltpu.VMEM((2, rows + PAD, 128), jnp.float32),
            pltpu.VMEM((4, 128 + 16, 128), jnp.float32),
        ],
        input_output_aliases={4: 0},
        compiler_params=pltpu.CompilerParams(vmem_limit_bytes=VMEM_LIMIT),
        cost_estimate=pl.CostEstimate(flops=0, bytes_accessed=8 * 2**20, transcendentals=0),
    )(om, of, back, sel, out)


def per_device(queries, keys, values, offset_mid, offset_far):
    args = (offset_mid, offset_far, queries, keys, values)
    send = pick(*args)
    got = lax.all_to_all(send, "inner", 0, 0)
    out, sel = local(0, PARTS[0], *args)
    got, out, sel = lax.optimization_barrier((got, out, sel))
    outer = lax.axis_size("outer")
    far = got[:, 128:136, 64:192].reshape(128, 128)
    far = lax.all_to_all(jnp.broadcast_to(far, (outer, 128, 128)), "outer", 0, 0)
    out, sel = local(PARTS[0], PARTS[1], *args, out, sel)
    far, out, sel = lax.optimization_barrier((far, out, sel))
    slot = lax.axis_index("inner").reshape(1)
    back = lax.all_to_all(cross(offset_mid.shape[0], slot, got, far), "inner", 0, 0)
    out, sel = local(PARTS[0] + PARTS[1], PARTS[2], *args, out, sel)
    return merge(offset_mid, offset_far, back, sel, out)


def solution(mesh):
    split = P(("outer", "inner"), None)
    return jax.shard_map(
        per_device,
        mesh=mesh,
        in_specs=(split, split, split, P(), P()),
        out_specs=split,
        check_vma=False,
    )
```
